32 devices in a mesh: sec: 4 (over y, x), row: 2 (over core), col: 4 (over z).
Axes of the slice: x: 2, y: 2, z: 4, core: 2. Of those that a mesh axis runs over, the one named last changes fastest.
Arguments:
- rhs: float32 [4, 8192, 256], P('sec', ('row', 'col')), may hold values from -6 to 6
- inv_factor: float32 [4, 8192, 8192], P('sec', 'col', 'row')
- coupling: float32 [4, 8192, 8192], P('sec', 'row', 'col'), may hold values from -0.0625 to 0.0625
- pattern: int32 [4, 64, 64], P('sec', 'row', 'col'), may hold values 0 or 1
Outputs:
- solution: float32 [4, 8192, 256], P('sec', 'col')
- outgoing: float32 [4, 8192, 256], P('sec', ('row', 'col'))
The draws below stay inside these ranges and needn't reach their ends.
All inputs are finite; a program needn't handle non-finite values. No bound on the sum of `pattern` on one device may be relied on, other than what follows from the above.
Results may differ from the reference program's by a relative error of at most 0.0001.
Values sent between devices are 32-bit elements; how exact they have to be, the bound alone decides.
No kernel may reach another device: no remote copies, remote signals or barrier semaphores. Data moves between devices by JAX's collectives and lax.ppermute only.
A program may use at most 192 MiB of HBM per device.

```python
import math
import jax
import jax.numpy as jnp
from jax import lax

S = 8192
BLK = 128
NRHS = 256
BLOCKS = 64
N_SEC = 4


def draw_inv_factor(key, part):
    shape = (N_SEC, S, S)
    noise = jax.random.normal(key, shape, jnp.float32)
    lower = jnp.tril(noise, -1) * (1.5 / math.sqrt(S))
    return lower + jnp.eye(S, dtype=jnp.float32)


def place_ends(result, key, least, top_value):
    spot = [jax.random.randint(jax.random.fold_in(key, axis), (), 0, length) for axis, length in enumerate(result.shape)]
    longest = result.shape.index(max(result.shape))
    next_to = spot[:longest] + [(spot[longest] + 1) % result.shape[longest]] + spot[longest + 1:]
    return result.at[tuple(spot)].set(least).at[tuple(next_to)].set(top_value)


def block_scale(rng, dims, shards, low, high):
    def one(position, blocks):
        heights = jax.random.uniform(jax.random.fold_in(jax.random.fold_in(rng, 6), position), (blocks,), jnp.float32, low / len(shards), high / len(shards))
        return jnp.repeat(jnp.exp(heights), dims[position] // blocks).reshape((-1,) + (1,) * (len(dims) - position - 1))

    gain = one(*shards[0])
    for cut in shards[1:]:
        gain = gain * one(*cut)
    return gain


def centred(rng, extent, deviation, reach, split=(), kind=jnp.bfloat16):
    drawn = deviation * jax.random.normal(rng, extent, jnp.float32)
    if split:
        drawn = drawn * block_scale(rng, extent, split, -0.22, 0.18)
    return jnp.clip(drawn, -reach, reach).astype(kind)


def setup_inputs(seed: int = 0) -> dict:
    key_list = jax.random.split(jax.random.key(seed), 5)
    return {
        "rhs": centred(key_list[0], (N_SEC, S, NRHS), 1.0, 6.0, ((0, 4), (1, 8)), jnp.float32),
        "inv_factor": draw_inv_factor(jax.random.fold_in(key_list[4], 71), 0),
        "coupling": centred(key_list[2], (N_SEC, S, S), S ** -0.5, 0.0625, ((0, 4), (1, 2), (2, 4)), jnp.float32),
        "pattern": place_ends((jax.random.randint(key_list[3], (N_SEC, BLOCKS, BLOCKS), 0, 20) < 17).astype(jnp.int32), jax.random.fold_in(key_list[3], 1), 0, 1),
    }


def masked_panel(coupling, pattern, section):
    occupancy = pattern[section].astype(jnp.float32)
    blocks = occupancy.shape[0]
    panel = coupling[section].reshape(blocks, BLK, blocks, BLK) * occupancy[:, None, :, None]
    return panel.reshape(S, S)


def reference(rhs, inv_factor, coupling, pattern):
    highest = lax.Precision.HIGHEST
    solved_list = []
    sends = []
    parent_rhs = rhs[N_SEC - 1]
    for section in range(N_SEC - 1):
        solved = jnp.dot(inv_factor[section], rhs[section], precision=highest, preferred_element_type=jnp.float32)
        update = jnp.dot(masked_panel(coupling, pattern, section), solved, precision=highest, preferred_element_type=jnp.float32)
        parent_rhs = parent_rhs - update
        solved_list.append(solved)
        sends.append(update)
    solved = jnp.dot(inv_factor[N_SEC - 1], parent_rhs, precision=highest, preferred_element_type=jnp.float32)
    update = jnp.dot(masked_panel(coupling, pattern, N_SEC - 1), solved, precision=highest, preferred_element_type=jnp.float32)
    solved_list.append(solved)
    sends.append(update)
    return jnp.stack(solved_list), jnp.stack(sends)
```

```python
import functools

import jax
import jax.numpy as jnp
from jax import lax
from jax.experimental import pallas as pl
from jax.experimental.pallas import tpu as pltpu
from jax.sharding import PartitionSpec as P

F32 = jnp.float32
BF16 = jnp.bfloat16
AXES = ("sec", "col")
VMEM_LIMIT = 20 * 1024 * 1024
AT_END, ORDER, SHARD = 2, 3, 7
COST = pl.CostEstimate(flops=1, bytes_accessed=1, transcendentals=0)


def split_words(value):
    high = value.astype(BF16)
    low = (value - high.astype(F32)).astype(BF16)
    return high, low


def three_term(tile, words, width):
    high, low = split_words(tile)
    both = jnp.dot(high, words, preferred_element_type=F32) + jnp.dot(low, words, preferred_element_type=F32)
    return both[:, :width] + both[:, width:]


def pieces_body(role, pieces_at, counts, started, meta, factor_ref, *refs):
    n_ops = sum(counts)
    ops, refs = refs[:n_ops], refs[n_ops:]
    if started:
        total_ref, refs = refs[0], refs[1:]
    out_ref, panel, held, words, sums, panel_sem, op_sem, sum_sem, out_sem = refs
    pieces = len(counts)
    slots, tile, joined = panel.shape
    tiles = factor_ref.shape[0] // tile
    depth, width = joined // pieces, held.shape[2]

    @pl.when(meta[role] == 1)
    def _():
        def tile_copy(p, t):
            column = meta[ORDER + pieces_at[p]] * depth
            return pltpu.make_async_copy(
                factor_ref.at[
                    pl.ds(pl.multiple_of(t * tile, tile), tile),
                    pl.ds(pl.multiple_of(column, depth), depth),
                ],
                panel.at[t % slots, :, pl.ds(p * depth, depth)],
                panel_sem.at[p, t % slots],
            )

        at = 0
        for p, count in enumerate(counts):
            group = [pltpu.make_async_copy(ops[at + k], held.at[p], op_sem.at[p]) for k in range(count)]
            at += count
            if count == 1:
                group[0].start()
            else:

                @pl.when(meta[AT_END] == 0)
                def _():
                    group[0].start()

                @pl.when(meta[AT_END] == 1)
                def _():
                    group[1].start()

        if started:
            sum_copy = pltpu.make_async_copy(total_ref, sums, sum_sem)
            sum_copy.start()
        for t in range(slots):
            for p in range(pieces):
                tile_copy(p, t).start()
        for p in range(pieces):
            pltpu.make_async_copy(ops[0], held.at[p], op_sem.at[p]).wait()
            high, low = split_words(held[p])
            words[p * depth : (p + 1) * depth, :width] = high
            words[p * depth : (p + 1) * depth, width:] = low
        if started:
            sum_copy.wait()

        def out_copy(t):
            rows = pl.ds(pl.multiple_of(t * tile, tile), tile)
            return pltpu.make_async_copy(sums.at[rows], out_ref.at[rows], out_sem.at[t])

        @pl.loop(0, tiles)
        def _(t):
            rows = pl.ds(pl.multiple_of(t * tile, tile), tile)
            for p in range(pieces):
                tile_copy(p, t).wait()
            value = three_term(panel[t % slots], words[...], width)
            sums[rows, :] = value + sums[rows, :] if started else value
            out_copy(t).start()

            @pl.when(t + slots < tiles)
            def _():
                for p in range(pieces):
                    tile_copy(p, t + slots).start()

        for t in range(tiles):
            out_copy(t).wait()


def factor_pieces(role, meta, pieces_at, factor, operands, total):
    rows = factor.shape[0]
    depth, width = operands[0][0].shape
    counts = tuple(len(group) for group in operands)
    n_pieces = len(counts)
    tile = min(rows, 256)
    tiles = rows // tile
    started = total is not None
    slots = min(tiles, 4)
    flat = [ref for group in operands for ref in group] + ([total] if started else [])
    anywhere = pl.BlockSpec(memory_space=pl.ANY)
    return pl.pallas_call(
        functools.partial(pieces_body, role, pieces_at, counts, started),
        out_shape=jax.ShapeDtypeStruct((rows, width), F32),
        in_specs=[pl.BlockSpec(memory_space=pltpu.SMEM)] + [anywhere] * (1 + len(flat)),
        out_specs=anywhere,
        scratch_shapes=[
            pltpu.VMEM((slots, tile, n_pieces * depth), F32),
            pltpu.VMEM((n_pieces, depth, width), F32),
            pltpu.VMEM((n_pieces * depth, 2 * width), BF16),
            pltpu.VMEM((rows, width), F32),
            pltpu.SemaphoreType.DMA((n_pieces, slots)),
            pltpu.SemaphoreType.DMA((n_pieces,)),
            pltpu.SemaphoreType.DMA,
            pltpu.SemaphoreType.DMA((tiles,)),
        ],
        compiler_params=pltpu.CompilerParams(vmem_limit_bytes=VMEM_LIMIT),
        cost_estimate=COST,
    )(meta, factor, *flat)


def masked_terms(panel, mask_ref, words, base, block_rows, width):
    parts = []
    for j in range(panel.shape[0] // block_rows):
        block = panel[j * block_rows : (j + 1) * block_rows, :] * mask_ref[pl.ds(base + j, 1), :]
        parts.append(three_term(block, words, width))
    return parts


def first_body(
    role, meta, panel_ref, mask_ref, mine_ref, other_ref, solved_ref, words_ref, out_ref,
    panel, mask, held, words, sums, panel_sem, in_sem, solved_sem, words_sem, out_sem,
):
    tiles, tile, depth = panel.shape
    width = held.shape[2]
    block_rows = panel_ref.shape[0] // mask_ref.shape[0]
    per = tile // block_rows

    @pl.when(meta[role] == 1)
    def _():
        def tile_copy(t):
            rows = pl.ds(pl.multiple_of((meta[SHARD] * tiles + t) * tile, tile), tile)
            return pltpu.make_async_copy(panel_ref.at[rows], panel.at[t], panel_sem.at[t])

        def out_copy(t):
            rows = pl.ds(pl.multiple_of(t * tile, tile), tile)
            return pltpu.make_async_copy(sums.at[rows], out_ref.at[rows], out_sem.at[t])

        inputs = [
            pltpu.make_async_copy(mine_ref, held.at[0], in_sem.at[0]),
            pltpu.make_async_copy(other_ref, held.at[1], in_sem.at[1]),
            pltpu.make_async_copy(mask_ref, mask, in_sem.at[2]),
        ]
        for copy in inputs:
            copy.start()
        for t in range(tiles):
            tile_copy(t).start()
        for copy in inputs:
            copy.wait()
        solved = held[0] + held[1]
        held[0] = solved
        high, low = split_words(solved)
        words[:, :width] = high
        words[:, width:] = low
        solved_copy = pltpu.make_async_copy(held.at[0], solved_ref, solved_sem)
        words_copy = pltpu.make_async_copy(words, words_ref, words_sem)

        @pl.loop(0, tiles)
        def _(t):
            tile_copy(t).wait()
            parts = masked_terms(panel[t], mask, words[...], (meta[SHARD] * tiles + t) * per, block_rows, width)
            for j, part in enumerate(parts):
                sums[pl.ds(pl.multiple_of(t * tile + j * block_rows, block_rows), block_rows), :] = part
            out_copy(t).start()

        solved_copy.start()
        words_copy.start()
        for t in range(tiles):
            out_copy(t).wait()
        solved_copy.wait()
        words_copy.wait()


def panel_first(role, meta, n, panel, mask, mine, other):
    depth, width = mine.shape
    rows = panel.shape[0] // n
    tile = min(rows, 256)
    tiles = rows // tile
    anywhere = pl.BlockSpec(memory_space=pl.ANY)
    return pl.pallas_call(
        functools.partial(first_body, role),
        out_shape=(
            jax.ShapeDtypeStruct((depth, width), F32),
            jax.ShapeDtypeStruct((depth, 2 * width), BF16),
            jax.ShapeDtypeStruct((rows, width), F32),
        ),
        in_specs=[pl.BlockSpec(memory_space=pltpu.SMEM)] + [anywhere] * 4,
        out_specs=(anywhere,) * 3,
        scratch_shapes=[
            pltpu.VMEM((tiles, tile, depth), F32),
            pltpu.VMEM(mask.shape, F32),
            pltpu.VMEM((2, depth, width), F32),
            pltpu.VMEM((depth, 2 * width), BF16),
            pltpu.VMEM((rows, width), F32),
            pltpu.SemaphoreType.DMA((tiles,)),
            pltpu.SemaphoreType.DMA((3,)),
            pltpu.SemaphoreType.DMA,
            pltpu.SemaphoreType.DMA,
            pltpu.SemaphoreType.DMA((tiles,)),
        ],
        compiler_params=pltpu.CompilerParams(vmem_limit_bytes=VMEM_LIMIT),
        cost_estimate=COST,
    )(meta, panel, mask, mine, other)


def rest_body(role, meta, panel_ref, mask_ref, words_ref, *refs):
    n_out = len(refs) - 7
    outs = refs[:n_out]
    panel, mask, words, sums, panel_sem, in_sem, out_sem = refs[n_out:]
    slots, tile, depth = panel.shape
    width = words.shape[1] // 2
    rows = outs[0].shape[0]
    tiles = rows // tile
    block_rows = panel_ref.shape[0] // mask_ref.shape[0]
    per = tile // block_rows

    @pl.when(meta[role] == 1)
    def _():
        def tile_copy(k, t):
            at = pl.ds(pl.multiple_of((meta[SHARD + 1 + k] * tiles + t) * tile, tile), tile)
            slot = (k * tiles + t) % slots
            return pltpu.make_async_copy(panel_ref.at[at], panel.at[slot], panel_sem.at[slot])

        def out_copy(k, t):
            at = pl.ds(pl.multiple_of(t * tile, tile), tile)
            return pltpu.make_async_copy(sums.at[k, at], outs[k].at[at], out_sem.at[k, t])

        inputs = [
            pltpu.make_async_copy(words_ref, words, in_sem.at[0]),
            pltpu.make_async_copy(mask_ref, mask, in_sem.at[1]),
        ]
        for copy in inputs:
            copy.start()
        for n in range(slots):
            tile_copy(n // tiles, n % tiles).start()
        for copy in inputs:
            copy.wait()
        for k in range(n_out):

            @pl.loop(0, tiles)
            def _(t):
                tile_copy(k, t).wait()
                slot = (k * tiles + t) % slots
                parts = masked_terms(panel[slot], mask, words[...], (meta[SHARD + 1 + k] * tiles + t) * per, block_rows, width)
                for j, part in enumerate(parts):
                    sums[k, pl.ds(pl.multiple_of(t * tile + j * block_rows, block_rows), block_rows), :] = part
                out_copy(k, t).start()
                ahead = k + slots // tiles
                if ahead < n_out:
                    tile_copy(ahead, t).start()

        for k in range(n_out):
            for t in range(tiles):
                out_copy(k, t).wait()


def panel_rest(role, meta, n, panel, mask, words):
    depth, wide = words.shape
    width = wide // 2
    rows = panel.shape[0] // n
    tile = min(rows, 256)
    tiles = rows // tile
    anywhere = pl.BlockSpec(memory_space=pl.ANY)
    return pl.pallas_call(
        functools.partial(rest_body, role),
        out_shape=tuple(jax.ShapeDtypeStruct((rows, width), F32) for _ in range(n - 1)),
        in_specs=[pl.BlockSpec(memory_space=pltpu.SMEM)] + [anywhere] * 3,
        out_specs=(anywhere,) * (n - 1),
        scratch_shapes=[
            pltpu.VMEM((tiles, tile, depth), F32),
            pltpu.VMEM(mask.shape, F32),
            pltpu.VMEM((depth, wide), BF16),
            pltpu.VMEM((n - 1, rows, width), F32),
            pltpu.SemaphoreType.DMA((tiles,)),
            pltpu.SemaphoreType.DMA((2,)),
            pltpu.SemaphoreType.DMA((n - 1, tiles)),
        ],
        compiler_params=pltpu.CompilerParams(vmem_limit_bytes=VMEM_LIMIT),
        cost_estimate=COST,
    )(meta, panel, mask, words)


def send(value, secs, pairs):
    n = lax.axis_size("col")
    return lax.ppermute(value, AXES, [(s * n + a, s * n + b) for s in secs for a, b in pairs])


def hop(value, pairs):
    n = lax.axis_size("col")
    return lax.ppermute(value, AXES, [(a * n + c, b * n + c) for a, b in pairs for c in range(n)])


EDGES = ((0, 1), (1, 0), (2, 3), (3, 2))
MIDDLE = ((1, 2), (2, 1))
INWARD = ((1, 0), (2, 3))
OUTWARD = ((0, 1), (3, 2))
ARRIVE = ((0, 1, 2, 3), (1, 0, 2, 3), (2, 3, 1, 0), (3, 2, 1, 0))
LEAVE = ((3, 2, 1, 0), (3, 2, 0, 1), (0, 1, 3, 2), (0, 1, 2, 3))


class Order:
    def __init__(self):
        self.noted = ()

    def step(self, *operands):
        tied = lax.optimization_barrier((*operands, *self.noted))
        self.noted = ()
        return tied[: len(operands)]

    def note(self, *results):
        self.noted += results
        return results if len(results) > 1 else results[0]


class Line:
    def __init__(self, role, secs, meta, inner, factor, panel, mask):
        self.role, self.secs, self.meta, self.inner = role, secs, meta, inner
        self.factor, self.panel, self.mask = factor, panel, mask

    def send(self, value, pairs):
        return send(value, self.secs, pairs)

    def solve(self, pieces_at, operands, total):
        return factor_pieces(self.role, self.meta, pieces_at, self.factor, operands, total)

    def swap(self, value):
        return lax.ppermute(value, "row", [(0, 1), (1, 0)])

    def first(self, mine, other):
        return panel_first(self.role, self.meta, len(LEAVE), self.panel, self.mask, mine, other)

    def rest(self, words):
        return panel_rest(self.role, self.meta, len(LEAVE), self.panel, self.mask, words)

    def both(self, inner, end):
        return jnp.where(self.inner, inner, end)

    def pair(self, own_a, own_b, passed):
        order = Order()
        side_a, mid_a = order.note(self.send(own_a, EDGES), self.send(own_a, MIDDLE))
        order.note(self.meta, self.mask)
        mid_a, side_a, self.meta, self.mask = order.step(mid_a, side_a, self.meta, self.mask)
        near_a, across_a = order.note(self.send(mid_a, INWARD), self.send(side_a, MIDDLE))
        own_a, side_a, mid_a, near_a, across_a = order.step(own_a, side_a, mid_a, near_a, across_a)
        far_a = order.note(self.send(across_a, INWARD))
        tot_a = order.note(self.solve((0, 1, 2), [[own_a], [side_a], [mid_a, near_a]], None))
        own_b, tot_a, across_a, far_a = order.step(own_b(), tot_a, across_a, far_a)
        side_b, mid_b = order.note(self.send(own_b, EDGES), self.send(own_b, MIDDLE))
        tot_a = self.solve((3,), [[across_a, far_a]], tot_a)
        solved_a, words_a, r0_a = order.note(*self.first(tot_a, self.swap(tot_a)))
        mid_b, side_b, r0_a, words_a = order.step(mid_b, side_b, r0_a, words_a)
        near_b, across_b = order.note(self.send(self.both(mid_b, r0_a), EDGES), self.send(side_b, MIDDLE))
        r1_a, r2_a, rown_a = order.note(*self.rest(words_a))
        across_b, r0_a, r1_a, near_b, own_b, side_b, mid_b = order.step(
            across_b, r0_a, r1_a, near_b, own_b, side_b, mid_b
        )
        far_b = order.note(self.send(self.both(across_b, r1_a), EDGES))
        got_a = order.note(self.send(r0_a + near_b, MIDDLE))
        tot_b = order.note(self.solve((0, 1, 2), [[own_b], [side_b], [mid_b, near_b]], None))
        r2_a, got_a, r1_a, far_b, tot_b, across_b = order.step(r2_a, got_a, r1_a, far_b, tot_b, across_b)
        rs_a, rm_a = order.note(self.send(r2_a + got_a, EDGES), self.send(r1_a + far_b, MIDDLE))
        tot_b = self.solve((3,), [[across_b, far_b]], tot_b)
        solved_b, words_b, r0_b = order.note(*self.first(tot_b, self.swap(tot_b)))
        r0_b, words_b, rown_a, rs_a, rm_a = order.step(r0_b, words_b, rown_a, rs_a, rm_a)
        sent_a = rown_a + rs_a + rm_a
        near = order.note(self.send(r0_b, OUTWARD))
        passed_a = order.note(passed(sent_a))
        r1_b, r2_b, rown_b = order.note(*self.rest(words_b))
        r0_b, near, r1_b = order.step(r0_b, near, r1_b)
        far, got = order.note(self.send(r1_b, OUTWARD), self.send(r0_b + near, MIDDLE))
        r2_b, got, r1_b, far = order.step(r2_b, got, r1_b, far)
        rs_b, rm_b = self.send(r2_b + got, EDGES), self.send(r1_b + far, MIDDLE)
        sent_b = rown_b + rs_b + rm_b
        return solved_a, sent_a, solved_b, sent_b, passed_a


def to_last(sent):
    top = lax.axis_size("sec") - 1
    total = hop(sent, ((0, top),))
    for s in range(1, top):
        total = total + hop(sent, ((s, top),))
    return total


def shards_line(rhs, inv_factor, coupling, pattern):
    top = lax.axis_size("sec") - 1
    factor, panel = inv_factor[0], coupling[0]
    mask = jnp.repeat(pattern[0].astype(F32), panel.shape[1] // pattern.shape[2], axis=1)
    is_parent = lax.axis_index("sec") == top
    col = lax.axis_index("col")
    inner = (col != 0) & (col != lax.axis_size("col") - 1)
    flags = jnp.stack([~is_parent, is_parent, ~inner]).astype(jnp.int32)
    orders = jnp.asarray([a + b for a, b in zip(ARRIVE, LEAVE)], jnp.int32)
    meta = jnp.concatenate([flags, orders[col]])
    kids = Line(0, tuple(range(top)), meta, inner, factor, panel, mask)
    half = rhs.shape[2] // 2
    own = [rhs[0][:, :half], rhs[0][:, half:]]
    solved0, sent0, solved1, sent1, passed0 = kids.pair(own[0], lambda: own[1], to_last)
    head = Line(1, (top,), kids.meta, inner, factor, panel, kids.mask)
    psolved0, psent0, psolved1, psent1, _ = head.pair(
        own[0] - passed0, lambda: own[1] - to_last(sent1), lambda sent: sent
    )
    pick = lambda p, c: jnp.where(is_parent, p, c)
    solution = jnp.concatenate([pick(psolved0, solved0), pick(psolved1, solved1)], axis=1)
    outgoing = jnp.concatenate([pick(psent0, sent0), pick(psent1, sent1)], axis=1)
    return solution[None], outgoing[None]


def shards_any(rhs, inv_factor, coupling, pattern):
    highest = lax.Precision.HIGHEST
    factor = inv_factor[0]
    coupling_local = coupling[0]
    occupancy = pattern[0].astype(jnp.float32)
    block_rows = coupling_local.shape[0] // occupancy.shape[0]
    block_cols = coupling_local.shape[1] // occupancy.shape[1]
    masked = (
        coupling_local.reshape(occupancy.shape[0], block_rows, occupancy.shape[1], block_cols)
        * occupancy[:, None, :, None]
    ).reshape(coupling_local.shape)
    parent_flag = lax.axis_index("sec") == lax.axis_size("sec") - 1

    def segment(rows):
        operand = lax.all_gather(rows, "col", axis=0, tiled=True)
        solved = lax.psum(jnp.dot(factor, operand, precision=highest, preferred_element_type=F32), "row")
        update = jnp.dot(masked, solved, precision=highest, preferred_element_type=F32)
        return solved, lax.psum_scatter(update, "col", scatter_dimension=0, tiled=True)

    solved_a, shares_a = segment(rhs[0])
    total = lax.psum(jnp.where(parent_flag, 0.0, shares_a), "sec")
    solved_b, shares_b = segment(rhs[0] - total)
    solution = jnp.where(parent_flag, solved_b, solved_a)
    outgoing = jnp.where(parent_flag, shares_b, shares_a)
    return (solution[None], outgoing[None])


def solution(mesh):
    placed = (
        P("sec", ("row", "col"), None),
        P("sec", "col", "row"),
        P("sec", "row", "col"),
        P("sec", "row", "col"),
    )
    line = mesh.shape["col"] == 4 and mesh.shape["row"] == 2 and mesh.shape["sec"] == 4
    return jax.shard_map(
        shards_line if line else shards_any,
        mesh=mesh,
        in_specs=placed,
        out_specs=(P("sec", "col", None), P("sec", ("row", "col"), None)),
        check_vma=False,
    )
```

```python
import functools

import jax
import jax.numpy as jnp
from jax import lax
from jax.experimental import pallas as pl
from jax.experimental.pallas import tpu as pltpu
from jax.sharding import PartitionSpec as P

F32 = jnp.float32
BF16 = jnp.bfloat16
AXES = ("sec", "col")
VMEM_LIMIT = 20 * 1024 * 1024
AT_END, ORDER, SHARD = 2, 3, 7
COST = pl.CostEstimate(flops=1, bytes_accessed=1, transcendentals=0)


def split_words(value):
    high = value.astype(BF16)
    low = (value - high.astype(F32)).astype(BF16)
    return high, low


def three_term(tile, words, width):
    high, low = split_words(tile)
    both = jnp.dot(high, words, preferred_element_type=F32) + jnp.dot(low, words, preferred_element_type=F32)
    return both[:, :width] + both[:, width:]


def pieces_body(role, pieces_at, counts, started, meta, factor_ref, *refs):
    n_ops = sum(counts)
    ops, refs = refs[:n_ops], refs[n_ops:]
    if started:
        total_ref, refs = refs[0], refs[1:]
    out_ref, panel, held, words, sums, panel_sem, op_sem, sum_sem, out_sem = refs
    pieces = len(counts)
    slots, tile, joined = panel.shape
    tiles = factor_ref.shape[0] // tile
    depth, width = joined // pieces, held.shape[2]

    @pl.when(meta[role] == 1)
    def _():
        def tile_copy(p, t):
            column = meta[ORDER + pieces_at[p]] * depth
            return pltpu.make_async_copy(
                factor_ref.at[
                    pl.ds(pl.multiple_of(t * tile, tile), tile),
                    pl.ds(pl.multiple_of(column, depth), depth),
                ],
                panel.at[t % slots, :, pl.ds(p * depth, depth)],
                panel_sem.at[p, t % slots],
            )

        at = 0
        for p, count in enumerate(counts):
            group = [pltpu.make_async_copy(ops[at + k], held.at[p], op_sem.at[p]) for k in range(count)]
            at += count
            if count == 1:
                group[0].start()
            else:

                @pl.when(meta[AT_END] == 0)
                def _():
                    group[0].start()

                @pl.when(meta[AT_END] == 1)
                def _():
                    group[1].start()

        if started:
            sum_copy = pltpu.make_async_copy(total_ref, sums, sum_sem)
            sum_copy.start()
        for t in range(slots):
            for p in range(pieces):
                tile_copy(p, t).start()
        for p in range(pieces):
            pltpu.make_async_copy(ops[0], held.at[p], op_sem.at[p]).wait()
            high, low = split_words(held[p])
            words[p * depth : (p + 1) * depth, :width] = high
            words[p * depth : (p + 1) * depth, width:] = low
        if started:
            sum_copy.wait()

        def out_copy(t):
            rows = pl.ds(pl.multiple_of(t * tile, tile), tile)
            return pltpu.make_async_copy(sums.at[rows], out_ref.at[rows], out_sem.at[t])

        @pl.loop(0, tiles)
        def _(t):
            rows = pl.ds(pl.multiple_of(t * tile, tile), tile)
            for p in range(pieces):
                tile_copy(p, t).wait()
            value = three_term(panel[t % slots], words[...], width)
            sums[rows, :] = value + sums[rows, :] if started else value
            out_copy(t).start()

            @pl.when(t + slots < tiles)
            def _():
                for p in range(pieces):
                    tile_copy(p, t + slots).start()

        for t in range(tiles):
            out_copy(t).wait()


def factor_pieces(role, meta, pieces_at, factor, operands, total):
    rows = factor.shape[0]
    depth, width = operands[0][0].shape
    counts = tuple(len(group) for group in operands)
    n_pieces = len(counts)
    tile = min(rows, 256)
    tiles = rows // tile
    started = total is not None
    slots = min(tiles, 4)
    flat = [ref for group in operands for ref in group] + ([total] if started else [])
    anywhere = pl.BlockSpec(memory_space=pl.ANY)
    return pl.pallas_call(
        functools.partial(pieces_body, role, pieces_at, counts, started),
        out_shape=jax.ShapeDtypeStruct((rows, width), F32),
        in_specs=[pl.BlockSpec(memory_space=pltpu.SMEM)] + [anywhere] * (1 + len(flat)),
        out_specs=anywhere,
        scratch_shapes=[
            pltpu.VMEM((slots, tile, n_pieces * depth), F32),
            pltpu.VMEM((n_pieces, depth, width), F32),
            pltpu.VMEM((n_pieces * depth, 2 * width), BF16),
            pltpu.VMEM((rows, width), F32),
            pltpu.SemaphoreType.DMA((n_pieces, slots)),
            pltpu.SemaphoreType.DMA((n_pieces,)),
            pltpu.SemaphoreType.DMA,
            pltpu.SemaphoreType.DMA((tiles,)),
        ],
        compiler_params=pltpu.CompilerParams(vmem_limit_bytes=VMEM_LIMIT),
        cost_estimate=COST,
    )(meta, factor, *flat)


def last_body(role, meta, block_ref, inner_ref, end_ref, total_ref, out_ref, held, words, sums, in_sem, out_sem):
    width = held.shape[1]
    tiles = out_sem.shape[0]
    tile = block_ref.shape[0] // tiles

    @pl.when(meta[role] == 1)
    def _():
        def out_copy(t):
            rows = pl.ds(pl.multiple_of(t * tile, tile), tile)
            return pltpu.make_async_copy(sums.at[rows], out_ref.at[rows], out_sem.at[t])

        @pl.when(meta[AT_END] == 0)
        def _():
            pltpu.make_async_copy(inner_ref, held, in_sem.at[0]).start()

        @pl.when(meta[AT_END] == 1)
        def _():
            pltpu.make_async_copy(end_ref, held, in_sem.at[0]).start()

        sum_copy = pltpu.make_async_copy(total_ref, sums, in_sem.at[1])
        sum_copy.start()
        pltpu.make_async_copy(end_ref, held, in_sem.at[0]).wait()
        high, low = split_words(held[...])
        words[:, :width] = high
        words[:, width:] = low
        sum_copy.wait()

        @pl.loop(0, tiles)
        def _(t):
            rows = pl.ds(pl.multiple_of(t * tile, tile), tile)
            sums[rows, :] = three_term(block_ref[rows, :], words[...], width) + sums[rows, :]
            out_copy(t).start()

        for t in range(tiles):
            out_copy(t).wait()


def last_piece(role, meta, block, inner, end, total):
    rows, depth = block.shape
    width = inner.shape[1]
    tiles = rows // min(rows, 512)
    anywhere = pl.BlockSpec(memory_space=pl.ANY)
    return pl.pallas_call(
        functools.partial(last_body, role),
        out_shape=jax.ShapeDtypeStruct((rows, width), F32),
        in_specs=[pl.BlockSpec(memory_space=pltpu.SMEM), pl.BlockSpec(memory_space=pltpu.VMEM)] + [anywhere] * 3,
        out_specs=anywhere,
        scratch_shapes=[
            pltpu.VMEM((depth, width), F32),
            pltpu.VMEM((depth, 2 * width), BF16),
            pltpu.VMEM((rows, width), F32),
            pltpu.SemaphoreType.DMA((2,)),
            pltpu.SemaphoreType.DMA((tiles,)),
        ],
        compiler_params=pltpu.CompilerParams(vmem_limit_bytes=VMEM_LIMIT),
        cost_estimate=COST,
    )(meta, block, inner, end, total)


def masked_terms(panel, mask_ref, words, base, block_rows, width):
    parts = []
    for j in range(panel.shape[0] // block_rows):
        block = panel[j * block_rows : (j + 1) * block_rows, :] * mask_ref[pl.ds(base + j, 1), :]
        parts.append(three_term(block, words, width))
    return parts


def first_body(
    role, meta, block_ref, mine_ref, other_ref, solved_ref, words_ref, out_ref,
    held, words, sums, in_sem, solved_sem, words_sem, out_sem,
):
    width = held.shape[2]
    tiles = out_sem.shape[0]
    tile = block_ref.shape[0] // tiles

    @pl.when(meta[role] == 1)
    def _():
        def out_copy(t):
            rows = pl.ds(pl.multiple_of(t * tile, tile), tile)
            return pltpu.make_async_copy(sums.at[rows], out_ref.at[rows], out_sem.at[t])

        inputs = [
            pltpu.make_async_copy(mine_ref, held.at[0], in_sem.at[0]),
            pltpu.make_async_copy(other_ref, held.at[1], in_sem.at[1]),
        ]
        for copy in inputs:
            copy.start()
        for copy in inputs:
            copy.wait()
        solved = held[0] + held[1]
        held[0] = solved
        high, low = split_words(solved)
        words[:, :width] = high
        words[:, width:] = low
        solved_copy = pltpu.make_async_copy(held.at[0], solved_ref, solved_sem)
        words_copy = pltpu.make_async_copy(words, words_ref, words_sem)
        solved_copy.start()
        words_copy.start()

        @pl.loop(0, tiles)
        def _(t):
            rows = pl.ds(pl.multiple_of(t * tile, tile), tile)
            sums[rows, :] = three_term(block_ref[rows, :], words[...], width)
            out_copy(t).start()

        for t in range(tiles):
            out_copy(t).wait()
        solved_copy.wait()
        words_copy.wait()


def panel_first(role, meta, block, mine, other):
    depth, width = mine.shape
    rows = block.shape[0]
    tiles = rows // min(rows, 256)
    anywhere = pl.BlockSpec(memory_space=pl.ANY)
    return pl.pallas_call(
        functools.partial(first_body, role),
        out_shape=(
            jax.ShapeDtypeStruct((depth, width), F32),
            jax.ShapeDtypeStruct((depth, 2 * width), BF16),
            jax.ShapeDtypeStruct((rows, width), F32),
        ),
        in_specs=[pl.BlockSpec(memory_space=pltpu.SMEM), pl.BlockSpec(memory_space=pltpu.VMEM)] + [anywhere] * 2,
        out_specs=(anywhere,) * 3,
        scratch_shapes=[
            pltpu.VMEM((2, depth, width), F32),
            pltpu.VMEM((depth, 2 * width), BF16),
            pltpu.VMEM((rows, width), F32),
            pltpu.SemaphoreType.DMA((2,)),
            pltpu.SemaphoreType.DMA,
            pltpu.SemaphoreType.DMA,
            pltpu.SemaphoreType.DMA((tiles,)),
        ],
        compiler_params=pltpu.CompilerParams(vmem_limit_bytes=VMEM_LIMIT),
        cost_estimate=COST,
    )(meta, block, mine, other)


def block_body(role, meta, block_ref, words_ref, out_ref, words, sums, in_sem, out_sem):
    width = sums.shape[1]
    tiles = out_sem.shape[0]
    tile = block_ref.shape[0] // tiles

    @pl.when(meta[role] == 1)
    def _():
        def out_copy(t):
            rows = pl.ds(pl.multiple_of(t * tile, tile), tile)
            return pltpu.make_async_copy(sums.at[rows], out_ref.at[rows], out_sem.at[t])

        words_copy = pltpu.make_async_copy(words_ref, words, in_sem)
        words_copy.start()
        words_copy.wait()

        @pl.loop(0, tiles)
        def _(t):
            rows = pl.ds(pl.multiple_of(t * tile, tile), tile)
            sums[rows, :] = three_term(block_ref[rows, :], words[...], width)
            out_copy(t).start()

        for t in range(tiles):
            out_copy(t).wait()


def panel_block(role, meta, block, words):
    depth, wide = words.shape
    rows = block.shape[0]
    tiles = rows // min(rows, 256)
    anywhere = pl.BlockSpec(memory_space=pl.ANY)
    return pl.pallas_call(
        functools.partial(block_body, role),
        out_shape=jax.ShapeDtypeStruct((rows, wide // 2), F32),
        in_specs=[pl.BlockSpec(memory_space=pltpu.SMEM), pl.BlockSpec(memory_space=pltpu.VMEM), anywhere],
        out_specs=anywhere,
        scratch_shapes=[
            pltpu.VMEM((depth, wide), BF16),
            pltpu.VMEM((rows, wide // 2), F32),
            pltpu.SemaphoreType.DMA,
            pltpu.SemaphoreType.DMA((tiles,)),
        ],
        compiler_params=pltpu.CompilerParams(vmem_limit_bytes=VMEM_LIMIT),
        cost_estimate=COST,
    )(meta, block, words)


def rest_body(role, ahead, meta, panel_ref, mask_ref, words_ref, *refs):
    n_out = len(refs) - 7
    outs = refs[:n_out]
    panel, mask, words, sums, panel_sem, in_sem, out_sem = refs[n_out:]
    slots, tile, depth = panel.shape
    width = words.shape[1] // 2
    rows = outs[0].shape[0]
    tiles = rows // tile
    block_rows = panel_ref.shape[0] // mask_ref.shape[0]
    per = tile // block_rows

    @pl.when(meta[role] == 1)
    def _():
        def tile_copy(k, t):
            at = pl.ds(pl.multiple_of((meta[SHARD + ahead + k] * tiles + t) * tile, tile), tile)
            slot = (k * tiles + t) % slots
            return pltpu.make_async_copy(panel_ref.at[at], panel.at[slot], panel_sem.at[slot])

        def out_copy(k, t):
            at = pl.ds(pl.multiple_of(t * tile, tile), tile)
            return pltpu.make_async_copy(sums.at[k, at], outs[k].at[at], out_sem.at[k, t])

        inputs = [
            pltpu.make_async_copy(words_ref, words, in_sem.at[0]),
            pltpu.make_async_copy(mask_ref, mask, in_sem.at[1]),
        ]
        for copy in inputs:
            copy.start()
        for n in range(slots):
            tile_copy(n // tiles, n % tiles).start()
        for copy in inputs:
            copy.wait()
        for k in range(n_out):

            @pl.loop(0, tiles)
            def _(t):
                tile_copy(k, t).wait()
                slot = (k * tiles + t) % slots
                base = (meta[SHARD + ahead + k] * tiles + t) * per
                for j, part in enumerate(masked_terms(panel[slot], mask, words[...], base, block_rows, width)):
                    at = pl.multiple_of(t * tile + j * block_rows, block_rows)
                    sums[k, pl.ds(at, block_rows), :] = part
                out_copy(k, t).start()
                if k + slots // tiles < n_out:
                    tile_copy(k + slots // tiles, t).start()

        for k in range(n_out):
            for t in range(tiles):
                out_copy(k, t).wait()


def panel_rest(role, meta, n, ahead, panel, mask, words):
    depth, wide = words.shape
    width = wide // 2
    rows = panel.shape[0] // n
    tile = min(rows, 256)
    tiles = rows // tile
    anywhere = pl.BlockSpec(memory_space=pl.ANY)
    return pl.pallas_call(
        functools.partial(rest_body, role, ahead),
        out_shape=tuple(jax.ShapeDtypeStruct((rows, width), F32) for _ in range(n - ahead)),
        in_specs=[pl.BlockSpec(memory_space=pltpu.SMEM)] + [anywhere] * 3,
        out_specs=(anywhere,) * (n - ahead),
        scratch_shapes=[
            pltpu.VMEM((tiles, tile, depth), F32),
            pltpu.VMEM(mask.shape, F32),
            pltpu.VMEM((depth, wide), BF16),
            pltpu.VMEM((n - ahead, rows, width), F32),
            pltpu.SemaphoreType.DMA((tiles,)),
            pltpu.SemaphoreType.DMA((2,)),
            pltpu.SemaphoreType.DMA((n - ahead, tiles)),
        ],
        compiler_params=pltpu.CompilerParams(vmem_limit_bytes=VMEM_LIMIT),
        cost_estimate=COST,
    )(meta, panel, mask, words)


def send(value, secs, pairs):
    n = lax.axis_size("col")
    return lax.ppermute(value, AXES, [(s * n + a, s * n + b) for s in secs for a, b in pairs])


def hop(value, pairs):
    n = lax.axis_size("col")
    return lax.ppermute(value, AXES, [(a * n + c, b * n + c) for a, b in pairs for c in range(n)])


EDGES = ((0, 1), (1, 0), (2, 3), (3, 2))
MIDDLE = ((1, 2), (2, 1))
INWARD = ((1, 0), (2, 3))
OUTWARD = ((0, 1), (3, 2))
ARRIVE = ((0, 1, 2, 3), (1, 0, 2, 3), (2, 3, 1, 0), (3, 2, 1, 0))
LEAVE = ((3, 2, 1, 0), (3, 2, 0, 1), (0, 1, 3, 2), (0, 1, 2, 3))


class Order:
    def __init__(self):
        self.noted = ()

    def step(self, *operands):
        tied = lax.optimization_barrier((*operands, *self.noted))
        self.noted = ()
        return tied[: len(operands)]

    def note(self, *results):
        self.noted += results
        return results if len(results) > 1 else results[0]


class Line:
    def __init__(self, role, secs, meta, inner, factor, panel, mask, blocks):
        self.role, self.secs, self.meta, self.inner = role, secs, meta, inner
        self.factor, self.panel, self.mask, self.blocks = factor, panel, mask, blocks

    def send(self, value, pairs):
        return send(value, self.secs, pairs)

    def solve(self, pieces_at, operands, total):
        return factor_pieces(self.role, self.meta, pieces_at, self.factor, operands, total)

    def swap(self, value):
        return lax.ppermute(value, "row", [(0, 1), (1, 0)])

    def last(self, inner, end, total):
        return last_piece(self.role, self.meta, self.blocks[0], inner, end, total)

    def first(self, mine, other):
        return panel_first(self.role, self.meta, self.blocks[1], mine, other)

    def rest(self, words):
        return panel_rest(self.role, self.meta, len(LEAVE), 2, self.panel, self.mask, words)

    def second(self, words):
        return panel_block(self.role, self.meta, self.blocks[2], words)

    def both(self, inner, end):
        return jnp.where(self.inner, inner, end)

    def pair(self, own_a, raw_b, to_b, passed):
        order = Order()
        side_a, mid_a = order.note(self.send(own_a, EDGES), self.send(own_a, MIDDLE))
        prepare = len(self.blocks) == 2
        if prepare:
            late, early = self.blocks
            late = late(self.meta)
            mid_a, side_a, self.meta, self.mask, late = order.step(mid_a, side_a, self.meta, self.mask, late)
            self.blocks = order.note(late, early(self.meta, self.mask, 0), early(self.meta, self.mask, 1))
        else:
            mid_a, side_a, own_a = order.step(mid_a, side_a, own_a)
        near_a, across_a = order.note(self.send(mid_a, INWARD), self.send(side_a, MIDDLE))
        tot_a = None if prepare else order.note(self.solve((0, 1), [[own_a], [side_a]], None))
        own_a, side_a, mid_a, near_a, across_a, raw_b = order.step(own_a, side_a, mid_a, near_a, across_a, raw_b)
        far_a = order.note(self.send(across_a, INWARD))
        if prepare:
            tot_a = order.note(self.solve((0, 1, 2), [[own_a], [side_a], [mid_a, near_a]], None))
        else:
            tot_a = order.note(self.solve((2,), [[mid_a, near_a]], tot_a))
        own_b, tot_a, across_a, far_a = order.step(to_b(raw_b), tot_a, across_a, far_a)
        side_b, mid_b = order.note(self.send(own_b, EDGES), self.send(own_b, MIDDLE))
        tot_a = self.last(across_a, far_a, tot_a)
        solved_a, words_a, r0_a = order.note(*self.first(tot_a, self.swap(tot_a)))
        mid_b, side_b, r0_a, words_a = order.step(mid_b, side_b, r0_a, words_a)
        near_b, across_b = order.note(self.send(self.both(mid_b, r0_a), EDGES), self.send(side_b, MIDDLE))
        r1_a = order.note(self.second(words_a))
        r2_a, rown_a = order.note(*self.rest(words_a))
        across_b, r0_a, r1_a, near_b, own_b, side_b, mid_b = order.step(
            across_b, r0_a, r1_a, near_b, own_b, side_b, mid_b
        )
        far_b = order.note(self.send(self.both(across_b, r1_a), EDGES))
        got_a = order.note(self.send(r0_a + near_b, MIDDLE))
        tot_b = order.note(self.solve((0, 1, 2), [[own_b], [side_b], [mid_b, near_b]], None))
        r2_a, got_a, r1_a, far_b, tot_b, across_b = order.step(r2_a, got_a, r1_a, far_b, tot_b, across_b)
        rs_a, rm_a = order.note(self.send(r2_a + got_a, EDGES), self.send(r1_a + far_b, MIDDLE))
        tot_b = self.last(across_b, far_b, tot_b)
        solved_b, words_b, r0_b = order.note(*self.first(tot_b, self.swap(tot_b)))
        r0_b, words_b, rown_a, rs_a, rm_a = order.step(r0_b, words_b, rown_a, rs_a, rm_a)
        sent_a = rown_a + rs_a + rm_a
        near = order.note(self.send(r0_b, OUTWARD))
        passed_a = passed(sent_a)
        r1_b = order.note(self.second(words_b))
        r0_b, near, r1_b, passed_a, words_b = order.step(r0_b, near, r1_b, passed_a, words_b)
        far, got = order.note(self.send(r1_b, OUTWARD), self.send(r0_b + near, MIDDLE))
        r2_b, rown_b = order.note(*self.rest(words_b))
        r2_b, got, r1_b, far = order.step(r2_b, got, r1_b, far)
        rs_b, rm_b = self.send(r2_b + got, EDGES), self.send(r1_b + far, MIDDLE)
        sent_b = rown_b + rs_b + rm_b
        return solved_a, sent_a, solved_b, sent_b, passed_a


def to_last(sent):
    half = sent.shape[0] // 2
    upper, lower = sent[:half], sent[half:]
    got_upper = hop(upper, ((0, 1), (2, 3)))
    got_lower = hop(lower, ((0, 2), (1, 3)))
    sum_upper = hop(upper + got_upper, ((1, 3),))
    sum_lower = hop(lower + got_lower, ((2, 3),))
    return jnp.concatenate([got_upper + sum_upper, got_lower + sum_lower], axis=0)


def shards_line(rhs, inv_factor, coupling, pattern):
    top = lax.axis_size("sec") - 1
    factor, panel = inv_factor[0], coupling[0]
    mask = jnp.repeat(pattern[0].astype(F32), panel.shape[1] // pattern.shape[2], axis=1)
    is_parent = lax.axis_index("sec") == top
    col = lax.axis_index("col")
    inner = (col != 0) & (col != lax.axis_size("col") - 1)
    flags = jnp.stack([~is_parent, is_parent, ~inner]).astype(jnp.int32)
    orders = jnp.asarray([a + b for a, b in zip(ARRIVE, LEAVE)], jnp.int32)
    meta = jnp.concatenate([flags, orders[col]])

    height = panel.shape[0] // len(LEAVE)
    per = height * mask.shape[0] // panel.shape[0]

    def late(meta):
        depth = rhs.shape[1]
        return lax.dynamic_slice(factor, (0, meta[ORDER + 3] * depth), (factor.shape[0], depth))

    def early(meta, mask, k):
        rows = lax.dynamic_slice(panel, (meta[SHARD + k] * height, 0), (height, panel.shape[1]))
        cover = lax.dynamic_slice(mask, (meta[SHARD + k] * per, 0), (per, panel.shape[1]))
        rows = rows.reshape(per, height // per, panel.shape[1]) * cover[:, None, :]
        return rows.reshape(height, panel.shape[1])

    kids = Line(0, tuple(range(top)), meta, inner, factor, panel, mask, (late, early))
    half = rhs.shape[2] // 2
    own = [rhs[0][:, :half], rhs[0][:, half:]]
    solved0, sent0, solved1, sent1, passed0 = kids.pair(own[0], own[1], lambda rows: rows, to_last)
    head = Line(1, (top,), kids.meta, inner, factor, panel, kids.mask, kids.blocks)
    psolved0, psent0, psolved1, psent1, _ = head.pair(
        own[0] - passed0, sent1, lambda sent: own[1] - to_last(sent), lambda sent: sent
    )
    pick = lambda p, c: jnp.where(is_parent, p, c)
    solution = jnp.concatenate([pick(psolved0, solved0), pick(psolved1, solved1)], axis=1)
    outgoing = jnp.concatenate([pick(psent0, sent0), pick(psent1, sent1)], axis=1)
    return solution[None], outgoing[None]


def shards_any(rhs, inv_factor, coupling, pattern):
    highest = lax.Precision.HIGHEST
    factor = inv_factor[0]
    coupling_local = coupling[0]
    occupancy = pattern[0].astype(jnp.float32)
    block_rows = coupling_local.shape[0] // occupancy.shape[0]
    block_cols = coupling_local.shape[1] // occupancy.shape[1]
    masked = (
        coupling_local.reshape(occupancy.shape[0], block_rows, occupancy.shape[1], block_cols)
        * occupancy[:, None, :, None]
    ).reshape(coupling_local.shape)
    parent_flag = lax.axis_index("sec") == lax.axis_size("sec") - 1

    def segment(rows):
        operand = lax.all_gather(rows, "col", axis=0, tiled=True)
        solved = lax.psum(jnp.dot(factor, operand, precision=highest, preferred_element_type=F32), "row")
        update = jnp.dot(masked, solved, precision=highest, preferred_element_type=F32)
        return solved, lax.psum_scatter(update, "col", scatter_dimension=0, tiled=True)

    solved_a, shares_a = segment(rhs[0])
    total = lax.psum(jnp.where(parent_flag, 0.0, shares_a), "sec")
    solved_b, shares_b = segment(rhs[0] - total)
    solution = jnp.where(parent_flag, solved_b, solved_a)
    outgoing = jnp.where(parent_flag, shares_b, shares_a)
    return (solution[None], outgoing[None])


def solution(mesh):
    placed = (
        P("sec", ("row", "col"), None),
        P("sec", "col", "row"),
        P("sec", "row", "col"),
        P("sec", "row", "col"),
    )
    line = mesh.shape["col"] == 4 and mesh.shape["row"] == 2 and mesh.shape["sec"] == 4
    return jax.shard_map(
        shards_line if line else shards_any,
        mesh=mesh,
        in_specs=placed,
        out_specs=(P("sec", "col", None), P("sec", ("row", "col"), None)),
        check_vma=False,
    )
```

```python
import functools

import jax
import jax.numpy as jnp
from jax import lax
from jax.experimental import pallas as pl
from jax.experimental.pallas import tpu as pltpu
from jax.sharding import PartitionSpec as P

F32 = jnp.float32
BF16 = jnp.bfloat16
AXES = ("sec", "col")
VMEM_LIMIT = 20 * 1024 * 1024
SWAPS = 3
AT_END, ORDER, SHARD = 2, 3, 7
COST = pl.CostEstimate(flops=1, bytes_accessed=1, transcendentals=0)


def split_words(value):
    high = value.astype(BF16)
    low = (value - high.astype(F32)).astype(BF16)
    return high, low


def three_term(tile, words, width):
    high, low = split_words(tile)
    both = jnp.dot(high, words, preferred_element_type=F32) + jnp.dot(low, words, preferred_element_type=F32)
    return both[:, :width] + both[:, width:]


IN_PLACE = pl.BlockSpec(memory_space=pltpu.VMEM)
ANYWHERE = pl.BlockSpec(memory_space=pl.ANY)
SCALARS = pl.BlockSpec(memory_space=pltpu.SMEM)
PARAMS = pltpu.CompilerParams(vmem_limit_bytes=VMEM_LIMIT)


def tiled(t, tile):
    return pl.ds(pl.multiple_of(t * tile, tile), tile)


def fill(words, at, values):
    rows, width = values.shape
    high, low = split_words(values)
    words[at : at + rows, :width] = high
    words[at : at + rows, width:] = low


def fill_for_chip(meta, words, at, refs):
    if len(refs) == 1:
        fill(words, at, refs[0][...])
    else:
        for end, ref in enumerate(refs):
            pl.when(meta[AT_END] == end)(lambda ref=ref: fill(words, at, ref[...]))


def pieces_body(role, pieces_at, counts, started, meta, factor_ref, *refs):
    n_ops = sum(counts)
    ops, refs = refs[:n_ops], refs[n_ops:]
    if started:
        total_ref, refs = refs[0], refs[1:]
    out_ref, panel, words, panel_sem = refs
    pieces = len(counts)
    slots, tile, joined = panel.shape
    tiles = factor_ref.shape[0] // tile
    depth, width = joined // pieces, out_ref.shape[1]

    @pl.when(meta[role] == 1)
    def _():
        def tile_copy(p, t):
            column = pl.multiple_of(meta[ORDER + pieces_at[p]] * depth, depth)
            return pltpu.make_async_copy(
                factor_ref.at[tiled(t, tile), pl.ds(column, depth)],
                panel.at[t % slots, :, pl.ds(p * depth, depth)],
                panel_sem.at[p, t % slots],
            )

        for t in range(slots):
            for p in range(pieces):
                tile_copy(p, t).start()
        at = 0
        for p, count in enumerate(counts):
            fill_for_chip(meta, words, p * depth, ops[at : at + count])
            at += count

        @pl.loop(0, tiles)
        def _(t):
            for p in range(pieces):
                tile_copy(p, t).wait()
            value = three_term(panel[t % slots], words[...], width)
            rows = tiled(t, tile)
            out_ref[rows, :] = value + total_ref[rows, :] if started else value

            @pl.when(t + slots < tiles)
            def _():
                for p in range(pieces):
                    tile_copy(p, t + slots).start()


def factor_pieces(role, meta, pieces_at, factor, operands, total):
    rows = factor.shape[0]
    depth, width = operands[0][0].shape
    counts = tuple(len(group) for group in operands)
    n_pieces = len(counts)
    tile = min(rows, 256)
    slots = min(rows // tile, 4)
    started = total is not None
    flat = [ref for group in operands for ref in group] + ([total] if started else [])
    return pl.pallas_call(
        functools.partial(pieces_body, role, pieces_at, counts, started),
        out_shape=jax.ShapeDtypeStruct((rows, width), F32),
        in_specs=[SCALARS, ANYWHERE] + [IN_PLACE] * len(flat),
        out_specs=IN_PLACE,
        scratch_shapes=[
            pltpu.VMEM((slots, tile, n_pieces * depth), F32),
            pltpu.VMEM((n_pieces * depth, 2 * width), BF16),
            pltpu.SemaphoreType.DMA((n_pieces, slots)),
        ],
        compiler_params=PARAMS,
        cost_estimate=COST,
    )(meta, factor, *flat)


def last_body(role, meta, block_ref, inner_ref, end_ref, total_ref, out_ref, words):
    rows, width = out_ref.shape
    tile = min(rows, 512)

    @pl.when(meta[role] == 1)
    def _():
        fill_for_chip(meta, words, 0, (inner_ref, end_ref))

        @pl.loop(0, rows // tile)
        def _(t):
            at = tiled(t, tile)
            out_ref[at, :] = three_term(block_ref[at, :], words[...], width) + total_ref[at, :]


def last_piece(role, meta, block, inner, end, total):
    depth, width = inner.shape
    return pl.pallas_call(
        functools.partial(last_body, role),
        out_shape=jax.ShapeDtypeStruct(total.shape, F32),
        in_specs=[SCALARS] + [IN_PLACE] * 4,
        out_specs=IN_PLACE,
        scratch_shapes=[pltpu.VMEM((depth, 2 * width), BF16)],
        compiler_params=PARAMS,
        cost_estimate=COST,
    )(meta, block, inner, end, total)


def masked_terms(panel, mask_ref, words, base, block_rows, width):
    parts = []
    for j in range(panel.shape[0] // block_rows):
        block = panel[j * block_rows : (j + 1) * block_rows, :] * mask_ref[pl.ds(base + j, 1), :]
        parts.append(three_term(block, words, width))
    return parts


def first_body(role, meta, block_ref, mine_ref, *refs):
    others, (solved_ref, words_ref, out_ref) = refs[:-3], refs[-3:]
    rows, width = out_ref.shape
    tile = min(rows, 512)

    @pl.when(meta[role] == 1)
    def _():
        at = 0
        for other in others:
            part = mine_ref[at : at + other.shape[0], :] + other[...]
            solved_ref[at : at + other.shape[0], :] = part
            fill(words_ref, at, part)
            at += other.shape[0]

        @pl.loop(0, rows // tile)
        def _(t):
            at = tiled(t, tile)
            out_ref[at, :] = three_term(block_ref[at, :], words_ref[...], width)


def panel_first(role, meta, block, mine, others):
    depth, width = mine.shape
    return pl.pallas_call(
        functools.partial(first_body, role),
        out_shape=(
            jax.ShapeDtypeStruct((depth, width), F32),
            jax.ShapeDtypeStruct((depth, 2 * width), BF16),
            jax.ShapeDtypeStruct((block.shape[0], width), F32),
        ),
        in_specs=[SCALARS] + [IN_PLACE] * (2 + len(others)),
        out_specs=(IN_PLACE,) * 3,
        compiler_params=PARAMS,
        cost_estimate=COST,
    )(meta, block, mine, *others)


def rest_body(role, ahead, blocks, meta, panel_ref, mask_ref, words_ref, *refs):
    block_refs, outs, (panel, panel_sem) = refs[:blocks], refs[blocks:-2], refs[-2:]
    n_out = len(outs)
    slots, tile, depth = panel.shape
    rows, width = outs[0].shape
    tiles = rows // tile
    block_rows = panel_ref.shape[0] // mask_ref.shape[0]
    per = tile // block_rows

    @pl.when(meta[role] == 1)
    def _():
        def tile_copy(k, t):
            at = tiled(meta[SHARD + ahead + k] * tiles + t, tile)
            slot = ((k - blocks) * tiles + t) % slots
            return pltpu.make_async_copy(panel_ref.at[at], panel.at[slot], panel_sem.at[slot])

        if n_out > blocks:
            for n in range(slots):
                tile_copy(blocks + n // tiles, n % tiles).start()
        for k in range(blocks):

            @pl.loop(0, tiles)
            def _(t):
                at = tiled(t, tile)
                outs[k][at, :] = three_term(block_refs[k][at, :], words_ref[...], width)

        for k in range(blocks, n_out):

            @pl.loop(0, tiles)
            def _(t):
                tile_copy(k, t).wait()
                slot = ((k - blocks) * tiles + t) % slots
                base = (meta[SHARD + ahead + k] * tiles + t) * per
                for j, part in enumerate(masked_terms(panel[slot], mask_ref, words_ref[...], base, block_rows, width)):
                    at = pl.multiple_of(t * tile + j * block_rows, block_rows)
                    outs[k][pl.ds(at, block_rows), :] = part
                if k + slots // tiles < n_out:
                    tile_copy(k + slots // tiles, t).start()


def panel_rest(role, meta, n, ahead, n_out, panel, mask, words, blocks):
    depth, wide = words.shape
    rows = panel.shape[0] // n
    tile = min(rows, 256)
    slots = rows // tile
    return pl.pallas_call(
        functools.partial(rest_body, role, ahead, len(blocks)),
        out_shape=tuple(jax.ShapeDtypeStruct((rows, wide // 2), F32) for _ in range(n_out)),
        in_specs=[SCALARS, ANYWHERE] + [IN_PLACE] * (2 + len(blocks)),
        out_specs=(IN_PLACE,) * n_out,
        scratch_shapes=[pltpu.VMEM((slots, tile, depth), F32), pltpu.SemaphoreType.DMA((slots,))],
        compiler_params=PARAMS,
        cost_estimate=COST,
    )(meta, panel, mask, words, *blocks)


def send(value, secs, pairs):
    n = lax.axis_size("col")
    return lax.ppermute(value, AXES, [(s * n + a, s * n + b) for s in secs for a, b in pairs])


def hop(value, pairs):
    n = lax.axis_size("col")
    return lax.ppermute(value, AXES, [(a * n + c, b * n + c) for a, b in pairs for c in range(n)])


EDGES = ((0, 1), (1, 0), (2, 3), (3, 2))
MIDDLE = ((1, 2), (2, 1))
INWARD = ((1, 0), (2, 3))
OUTWARD = ((0, 1), (3, 2))
ARRIVE = ((0, 1, 2, 3), (1, 0, 2, 3), (2, 3, 1, 0), (3, 2, 1, 0))
LEAVE = ((3, 2, 1, 0), (3, 2, 0, 1), (0, 1, 3, 2), (0, 1, 2, 3))


class Order:
    def __init__(self):
        self.noted = ()

    def step(self, *operands):
        tied = lax.optimization_barrier((*operands, *self.noted))
        self.noted = ()
        return tied[: len(operands)]

    def note(self, *results):
        self.noted += results
        return results if len(results) > 1 else results[0]


class Line:
    def __init__(self, role, secs, meta, inner, factor, panel, mask, blocks):
        self.role, self.secs, self.meta, self.inner = role, secs, meta, inner
        self.factor, self.panel, self.mask, self.blocks = factor, panel, mask, blocks

    def send(self, value, pairs):
        return send(value, self.secs, pairs)

    def solve(self, pieces_at, operands, total):
        return factor_pieces(self.role, self.meta, pieces_at, self.factor, operands, total)

    def swap(self, value):
        step = -(-value.shape[0] // (SWAPS * 16)) * 16
        parts = [value[at : at + step] for at in range(0, value.shape[0], step)]
        return [lax.ppermute(part, "row", [(0, 1), (1, 0)]) for part in parts]

    def last(self, inner, end, total):
        return last_piece(self.role, self.meta, self.blocks[0], inner, end, total)

    def first(self, mine, others):
        return panel_first(self.role, self.meta, self.blocks[1], mine, others)

    def rest(self, words, ahead, n_out, blocks):
        return panel_rest(self.role, self.meta, len(LEAVE), ahead, n_out, self.panel, self.mask, words, blocks)

    def both(self, inner, end):
        return jnp.where(self.inner, inner, end)

    def pair(self, own_a, raw_b, to_b, passed):
        order = Order()
        side_a, mid_a = order.note(self.send(own_a, EDGES), self.send(own_a, MIDDLE))
        prepare = len(self.blocks) == 2
        if prepare:
            late, early = self.blocks
            late = late(self.meta)
            mid_a, side_a, self.meta, self.mask, late = order.step(mid_a, side_a, self.meta, self.mask, late)
            self.blocks = order.note(late, early(self.meta, self.mask, 0), early(self.meta, self.mask, 1))
        else:
            mid_a, side_a, own_a = order.step(mid_a, side_a, own_a)
        near_a, across_a = order.note(self.send(mid_a, INWARD), self.send(side_a, MIDDLE))
        tot_a = None if prepare else order.note(self.solve((0, 1), [[own_a], [side_a]], None))
        own_a, side_a, mid_a, near_a, across_a, raw_b = order.step(own_a, side_a, mid_a, near_a, across_a, raw_b)
        far_a = order.note(self.send(across_a, INWARD))
        if prepare:
            tot_a = order.note(self.solve((0, 1, 2), [[own_a], [side_a], [mid_a, near_a]], None))
        else:
            tot_a = order.note(self.solve((2,), [[mid_a, near_a]], tot_a))
        own_b, tot_a, across_a, far_a = order.step(to_b(raw_b), tot_a, across_a, far_a)
        side_b, mid_b = order.note(self.send(own_b, EDGES), self.send(own_b, MIDDLE))
        tot_a = self.last(across_a, far_a, tot_a)
        solved_a, words_a, r0_a = order.note(*self.first(tot_a, self.swap(tot_a)))
        mid_b, side_b, r0_a, words_a = order.step(mid_b, side_b, r0_a, words_a)
        near_b, across_b = order.note(self.send(self.both(mid_b, r0_a), EDGES), self.send(side_b, MIDDLE))
        r1_a, r2_a, rown_a = order.note(*self.rest(words_a, 1, 3, self.blocks[2:]))
        across_b, r0_a, r1_a, near_b, own_b, side_b, mid_b = order.step(
            across_b, r0_a, r1_a, near_b, own_b, side_b, mid_b
        )
        far_b = order.note(self.send(self.both(across_b, r1_a), EDGES))
        got_a = order.note(self.send(r0_a + near_b, MIDDLE))
        tot_b = order.note(self.solve((0, 1, 2), [[own_b], [side_b], [mid_b, near_b]], None))
        r2_a, got_a, r1_a, far_b, tot_b, across_b = order.step(r2_a, got_a, r1_a, far_b, tot_b, across_b)
        rs_a, rm_a = order.note(self.send(r2_a + got_a, EDGES), self.send(r1_a + far_b, MIDDLE))
        tot_b = self.last(across_b, far_b, tot_b)
        solved_b, words_b, r0_b = order.note(*self.first(tot_b, self.swap(tot_b)))
        r0_b, words_b, rown_a, rs_a, rm_a = order.step(r0_b, words_b, rown_a, rs_a, rm_a)
        sent_a = rown_a + rs_a + rm_a
        near = order.note(self.send(r0_b, OUTWARD))
        passed_a = passed(sent_a)
        r1_b = order.note(*self.rest(words_b, 1, 1, self.blocks[2:]))
        r0_b, near, r1_b, passed_a, words_b = order.step(r0_b, near, r1_b, passed_a, words_b)
        far, got = order.note(self.send(r1_b, OUTWARD), self.send(r0_b + near, MIDDLE))
        r2_b, rown_b = order.note(*self.rest(words_b, 2, 2, ()))
        r2_b, got, r1_b, far = order.step(r2_b, got, r1_b, far)
        rs_b, rm_b = self.send(r2_b + got, EDGES), self.send(r1_b + far, MIDDLE)
        sent_b = rown_b + rs_b + rm_b
        return solved_a, sent_a, solved_b, sent_b, passed_a


def to_last(sent):
    half = sent.shape[0] // 2
    upper, lower = sent[:half], sent[half:]
    got_upper = hop(upper, ((0, 1), (2, 3)))
    got_lower = hop(lower, ((0, 2), (1, 3)))
    sum_upper = hop(upper + got_upper, ((1, 3),))
    sum_lower = hop(lower + got_lower, ((2, 3),))
    return jnp.concatenate([got_upper + sum_upper, got_lower + sum_lower], axis=0)


def shards_line(rhs, inv_factor, coupling, pattern):
    top = lax.axis_size("sec") - 1
    factor, panel = inv_factor[0], coupling[0]
    mask = jnp.repeat(pattern[0].astype(F32), panel.shape[1] // pattern.shape[2], axis=1)
    is_parent = lax.axis_index("sec") == top
    col = lax.axis_index("col")
    inner = (col != 0) & (col != lax.axis_size("col") - 1)
    flags = jnp.stack([~is_parent, is_parent, ~inner]).astype(jnp.int32)
    orders = jnp.asarray([a + b for a, b in zip(ARRIVE, LEAVE)], jnp.int32)
    meta = jnp.concatenate([flags, orders[col]])

    height = panel.shape[0] // len(LEAVE)
    per = height * mask.shape[0] // panel.shape[0]

    def late(meta):
        depth = rhs.shape[1]
        return lax.dynamic_slice(factor, (0, meta[ORDER + 3] * depth), (factor.shape[0], depth))

    def early(meta, mask, k):
        rows = lax.dynamic_slice(panel, (meta[SHARD + k] * height, 0), (height, panel.shape[1]))
        cover = lax.dynamic_slice(mask, (meta[SHARD + k] * per, 0), (per, panel.shape[1]))
        rows = rows.reshape(per, height // per, panel.shape[1]) * cover[:, None, :]
        return rows.reshape(height, panel.shape[1])

    kids = Line(0, tuple(range(top)), meta, inner, factor, panel, mask, (late, early))
    half = rhs.shape[2] // 2
    own = [rhs[0][:, :half], rhs[0][:, half:]]
    solved0, sent0, solved1, sent1, passed0 = kids.pair(own[0], own[1], lambda rows: rows, to_last)
    head = Line(1, (top,), kids.meta, inner, factor, panel, kids.mask, kids.blocks)
    psolved0, psent0, psolved1, psent1, _ = head.pair(
        own[0] - passed0, sent1, lambda sent: own[1] - to_last(sent), lambda sent: sent
    )
    pick = lambda p, c: jnp.where(is_parent, p, c)
    solution = jnp.concatenate([pick(psolved0, solved0), pick(psolved1, solved1)], axis=1)
    outgoing = jnp.concatenate([pick(psent0, sent0), pick(psent1, sent1)], axis=1)
    return solution[None], outgoing[None]


def shards_any(rhs, inv_factor, coupling, pattern):
    highest = lax.Precision.HIGHEST
    factor = inv_factor[0]
    coupling_local = coupling[0]
    occupancy = pattern[0].astype(jnp.float32)
    block_rows = coupling_local.shape[0] // occupancy.shape[0]
    block_cols = coupling_local.shape[1] // occupancy.shape[1]
    masked = (
        coupling_local.reshape(occupancy.shape[0], block_rows, occupancy.shape[1], block_cols)
        * occupancy[:, None, :, None]
    ).reshape(coupling_local.shape)
    parent_flag = lax.axis_index("sec") == lax.axis_size("sec") - 1

    def segment(rows):
        operand = lax.all_gather(rows, "col", axis=0, tiled=True)
        solved = lax.psum(jnp.dot(factor, operand, precision=highest, preferred_element_type=F32), "row")
        update = jnp.dot(masked, solved, precision=highest, preferred_element_type=F32)
        return solved, lax.psum_scatter(update, "col", scatter_dimension=0, tiled=True)

    solved_a, shares_a = segment(rhs[0])
    total = lax.psum(jnp.where(parent_flag, 0.0, shares_a), "sec")
    solved_b, shares_b = segment(rhs[0] - total)
    solution = jnp.where(parent_flag, solved_b, solved_a)
    outgoing = jnp.where(parent_flag, shares_b, shares_a)
    return (solution[None], outgoing[None])


def solution(mesh):
    placed = (
        P("sec", ("row", "col"), None),
        P("sec", "col", "row"),
        P("sec", "row", "col"),
        P("sec", "row", "col"),
    )
    line = mesh.shape["col"] == 4 and mesh.shape["row"] == 2 and mesh.shape["sec"] == 4
    return jax.shard_map(
        shards_line if line else shards_any,
        mesh=mesh,
        in_specs=placed,
        out_specs=(P("sec", "col", None), P("sec", ("row", "col"), None)),
        check_vma=False,
    )
```

```python
import functools

import jax
import jax.numpy as jnp
from jax import lax
from jax.experimental import pallas as pl
from jax.experimental.pallas import tpu as pltpu
from jax.sharding import PartitionSpec as P

F32 = jnp.float32
BF16 = jnp.bfloat16
AXES = ("sec", "col")
VMEM_LIMIT = 20 * 1024 * 1024
SWAPS = 3
AT_END, ORDER, SHARD = 2, 3, 7
COST = pl.CostEstimate(flops=1, bytes_accessed=1, transcendentals=0)


def split_words(value):
    high = value.astype(BF16)
    low = (value - high.astype(F32)).astype(BF16)
    return high, low


def three_term(tile, words, width):
    high, low = split_words(tile)
    both = jnp.dot(high, words, preferred_element_type=F32) + jnp.dot(low, words, preferred_element_type=F32)
    return both[:, :width] + both[:, width:]


IN_PLACE = pl.BlockSpec(memory_space=pltpu.VMEM)
ANYWHERE = pl.BlockSpec(memory_space=pl.ANY)
SCALARS = pl.BlockSpec(memory_space=pltpu.SMEM)
PARAMS = pltpu.CompilerParams(vmem_limit_bytes=VMEM_LIMIT)


def tiled(t, tile):
    return pl.ds(pl.multiple_of(t * tile, tile), tile)


def fill(words, at, values):
    rows, width = values.shape
    high, low = split_words(values)
    words[at : at + rows, :width] = high
    words[at : at + rows, width:] = low


def fill_for_chip(meta, words, at, refs):
    if len(refs) == 1:
        fill(words, at, refs[0][...])
    else:
        for end, ref in enumerate(refs):
            pl.when(meta[AT_END] == end)(lambda ref=ref: fill(words, at, ref[...]))


def pieces_body(role, pieces_at, counts, started, meta, factor_ref, *refs):
    n_ops = sum(counts)
    ops, refs = refs[:n_ops], refs[n_ops:]
    if started:
        total_ref, refs = refs[0], refs[1:]
    out_ref, panel, words, panel_sem = refs
    pieces = len(counts)
    slots, tile, joined = panel.shape
    tiles = factor_ref.shape[0] // tile
    depth, width = joined // pieces, out_ref.shape[1]

    @pl.when(meta[role] == 1)
    def _():
        def tile_copy(p, t):
            column = pl.multiple_of(meta[ORDER + pieces_at[p]] * depth, depth)
            return pltpu.make_async_copy(
                factor_ref.at[tiled(t, tile), pl.ds(column, depth)],
                panel.at[t % slots, :, pl.ds(p * depth, depth)],
                panel_sem.at[p, t % slots],
            )

        for t in range(slots):
            for p in range(pieces):
                tile_copy(p, t).start()
        at = 0
        for p, count in enumerate(counts):
            fill_for_chip(meta, words, p * depth, ops[at : at + count])
            at += count

        @pl.loop(0, tiles)
        def _(t):
            for p in range(pieces):
                tile_copy(p, t).wait()
            value = three_term(panel[t % slots], words[...], width)
            rows = tiled(t, tile)
            out_ref[rows, :] = value + total_ref[rows, :] if started else value

            @pl.when(t + slots < tiles)
            def _():
                for p in range(pieces):
                    tile_copy(p, t + slots).start()


def factor_pieces(role, meta, pieces_at, factor, operands, total):
    rows = factor.shape[0]
    depth, width = operands[0][0].shape
    counts = tuple(len(group) for group in operands)
    n_pieces = len(counts)
    tile = min(rows, 256)
    slots = min(rows // tile, 4)
    started = total is not None
    flat = [ref for group in operands for ref in group] + ([total] if started else [])
    return pl.pallas_call(
        functools.partial(pieces_body, role, pieces_at, counts, started),
        out_shape=jax.ShapeDtypeStruct((rows, width), F32),
        in_specs=[SCALARS, ANYWHERE] + [IN_PLACE] * len(flat),
        out_specs=IN_PLACE,
        scratch_shapes=[
            pltpu.VMEM((slots, tile, n_pieces * depth), F32),
            pltpu.VMEM((n_pieces * depth, 2 * width), BF16),
            pltpu.SemaphoreType.DMA((n_pieces, slots)),
        ],
        compiler_params=PARAMS,
        cost_estimate=COST,
    )(meta, factor, *flat)


def last_body(role, meta, block_ref, inner_ref, end_ref, total_ref, out_ref, words):
    rows, width = out_ref.shape
    tile = min(rows, 512)

    @pl.when(meta[role] == 1)
    def _():
        fill_for_chip(meta, words, 0, (inner_ref, end_ref))

        @pl.loop(0, rows // tile)
        def _(t):
            at = tiled(t, tile)
            out_ref[at, :] = three_term(block_ref[at, :], words[...], width) + total_ref[at, :]


def last_piece(role, meta, block, inner, end, total):
    depth, width = inner.shape
    return pl.pallas_call(
        functools.partial(last_body, role),
        out_shape=jax.ShapeDtypeStruct(total.shape, F32),
        in_specs=[SCALARS] + [IN_PLACE] * 4,
        out_specs=IN_PLACE,
        scratch_shapes=[pltpu.VMEM((depth, 2 * width), BF16)],
        compiler_params=PARAMS,
        cost_estimate=COST,
    )(meta, block, inner, end, total)


def masked_terms(panel, mask_ref, words, base, block_rows, width):
    parts = []
    for j in range(panel.shape[0] // block_rows):
        block = panel[j * block_rows : (j + 1) * block_rows, :] * mask_ref[pl.ds(base + j, 1), :]
        parts.append(three_term(block, words, width))
    return parts


def first_body(role, meta, block_ref, mine_ref, *refs):
    others, (solved_ref, words_ref, out_ref) = refs[:-3], refs[-3:]
    rows, width = out_ref.shape
    tile = min(rows, 512)

    @pl.when(meta[role] == 1)
    def _():
        at = 0
        for other in others:
            part = mine_ref[at : at + other.shape[0], :] + other[...]
            solved_ref[at : at + other.shape[0], :] = part
            fill(words_ref, at, part)
            at += other.shape[0]

        @pl.loop(0, rows // tile)
        def _(t):
            at = tiled(t, tile)
            out_ref[at, :] = three_term(block_ref[at, :], words_ref[...], width)


def panel_first(role, meta, block, mine, others):
    depth, width = mine.shape
    return pl.pallas_call(
        functools.partial(first_body, role),
        out_shape=(
            jax.ShapeDtypeStruct((depth, width), F32),
            jax.ShapeDtypeStruct((depth, 2 * width), BF16),
            jax.ShapeDtypeStruct((block.shape[0], width), F32),
        ),
        in_specs=[SCALARS] + [IN_PLACE] * (2 + len(others)),
        out_specs=(IN_PLACE,) * 3,
        compiler_params=PARAMS,
        cost_estimate=COST,
    )(meta, block, mine, *others)


def rest_body(role, ahead, blocks, meta, panel_ref, mask_ref, words_ref, *refs):
    block_refs, outs, (panel, panel_sem) = refs[:blocks], refs[blocks:-2], refs[-2:]
    n_out = len(outs)
    slots, tile, depth = panel.shape
    rows, width = outs[0].shape
    tiles = rows // tile
    block_rows = panel_ref.shape[0] // mask_ref.shape[0]
    per = tile // block_rows

    @pl.when(meta[role] == 1)
    def _():
        def tile_copy(k, t):
            at = tiled(meta[SHARD + ahead + k] * tiles + t, tile)
            slot = ((k - blocks) * tiles + t) % slots
            return pltpu.make_async_copy(panel_ref.at[at], panel.at[slot], panel_sem.at[slot])

        if n_out > blocks:
            for n in range(slots):
                tile_copy(blocks + n // tiles, n % tiles).start()
        for k in range(blocks):

            @pl.loop(0, tiles)
            def _(t):
                at = tiled(t, tile)
                outs[k][at, :] = three_term(block_refs[k][at, :], words_ref[...], width)

        for k in range(blocks, n_out):

            @pl.loop(0, tiles)
            def _(t):
                tile_copy(k, t).wait()
                slot = ((k - blocks) * tiles + t) % slots
                base = (meta[SHARD + ahead + k] * tiles + t) * per
                for j, part in enumerate(masked_terms(panel[slot], mask_ref, words_ref[...], base, block_rows, width)):
                    at = pl.multiple_of(t * tile + j * block_rows, block_rows)
                    outs[k][pl.ds(at, block_rows), :] = part
                if k + slots // tiles < n_out:
                    tile_copy(k + slots // tiles, t).start()


def panel_rest(role, meta, n, ahead, n_out, panel, mask, words, blocks):
    depth, wide = words.shape
    rows = panel.shape[0] // n
    tile = min(rows, 256)
    slots = rows // tile
    return pl.pallas_call(
        functools.partial(rest_body, role, ahead, len(blocks)),
        out_shape=tuple(jax.ShapeDtypeStruct((rows, wide // 2), F32) for _ in range(n_out)),
        in_specs=[SCALARS, ANYWHERE] + [IN_PLACE] * (2 + len(blocks)),
        out_specs=(IN_PLACE,) * n_out,
        scratch_shapes=[pltpu.VMEM((slots, tile, depth), F32), pltpu.SemaphoreType.DMA((slots,))],
        compiler_params=PARAMS,
        cost_estimate=COST,
    )(meta, panel, mask, words, *blocks)


def send(value, secs, pairs):
    n = lax.axis_size("col")
    return lax.ppermute(value, AXES, [(s * n + a, s * n + b) for s in secs for a, b in pairs])


def hop(value, pairs):
    n = lax.axis_size("col")
    return lax.ppermute(value, AXES, [(a * n + c, b * n + c) for a, b in pairs for c in range(n)])


EDGES = ((0, 1), (1, 0), (2, 3), (3, 2))
MIDDLE = ((1, 2), (2, 1))
INWARD = ((1, 0), (2, 3))
OUTWARD = ((0, 1), (3, 2))
ARRIVE = ((0, 1, 2, 3), (1, 0, 2, 3), (2, 3, 1, 0), (3, 2, 1, 0))
LEAVE = ((3, 2, 1, 0), (3, 2, 0, 1), (0, 1, 3, 2), (0, 1, 2, 3))


class Order:
    def __init__(self):
        self.noted = ()

    def step(self, *operands):
        tied = lax.optimization_barrier((*operands, *self.noted))
        self.noted = ()
        return tied[: len(operands)]

    def note(self, *results):
        self.noted += results
        return results if len(results) > 1 else results[0]


class Line:
    def __init__(self, role, secs, meta, inner, factor, panel, mask, blocks):
        self.role, self.secs, self.meta, self.inner = role, secs, meta, inner
        self.factor, self.panel, self.mask, self.blocks = factor, panel, mask, blocks

    def send(self, value, pairs):
        return send(value, self.secs, pairs)

    def solve(self, pieces_at, operands, total):
        return factor_pieces(self.role, self.meta, pieces_at, self.factor, operands, total)

    def swap(self, value):
        step = -(-value.shape[0] // (SWAPS * 16)) * 16
        parts = [value[at : at + step] for at in range(0, value.shape[0], step)]
        return [lax.ppermute(part, "row", [(0, 1), (1, 0)]) for part in parts]

    def last(self, inner, end, total):
        return last_piece(self.role, self.meta, self.blocks[0], inner, end, total)

    def first(self, mine, others):
        return panel_first(self.role, self.meta, self.blocks[1], mine, others)

    def rest(self, words, ahead, n_out, blocks):
        return panel_rest(self.role, self.meta, len(LEAVE), ahead, n_out, self.panel, self.mask, words, blocks)

    def send_first(self, value, pairs, more=16):
        rows = value.shape[0]
        return self.send(jnp.pad(value, ((0, more), (0, 0))), pairs)[:rows]

    def both(self, inner, end):
        return jnp.where(self.inner, inner, end)

    def pair(self, own_a, raw_b, to_b, passed):
        order = Order()
        side_a, mid_a = order.note(self.send(own_a, EDGES), self.send(own_a, MIDDLE))
        prepare = len(self.blocks) == 2
        if prepare:
            late, early = self.blocks
            late = late(self.meta)
            mid_a, side_a, self.meta, self.mask, late = order.step(mid_a, side_a, self.meta, self.mask, late)
            self.blocks = order.note(late, early(self.meta, self.mask, 0), early(self.meta, self.mask, 1))
        else:
            mid_a, side_a, own_a = order.step(mid_a, side_a, own_a)
        near_a, across_a = order.note(self.send_first(mid_a, INWARD), self.send(side_a, MIDDLE))
        tot_a = None if prepare else order.note(self.solve((0, 1), [[own_a], [side_a]], None))
        own_a, side_a, mid_a, near_a, across_a, raw_b = order.step(own_a, side_a, mid_a, near_a, across_a, raw_b)
        far_a = order.note(self.send(across_a, INWARD))
        if prepare:
            tot_a = order.note(self.solve((0, 1, 2), [[own_a], [side_a], [mid_a, near_a]], None))
        else:
            tot_a = order.note(self.solve((2,), [[mid_a, near_a]], tot_a))
        own_b, tot_a, across_a, far_a = order.step(to_b(raw_b), tot_a, across_a, far_a)
        side_b, mid_b = order.note(self.send(own_b, EDGES), self.send(own_b, MIDDLE))
        tot_a = self.last(across_a, far_a, tot_a)
        solved_a, words_a, r0_a = order.note(*self.first(tot_a, self.swap(tot_a)))
        mid_b, side_b, r0_a, words_a = order.step(mid_b, side_b, r0_a, words_a)
        near_b, across_b = order.note(self.send(self.both(mid_b, r0_a), EDGES), self.send(side_b, MIDDLE))
        r1_a, r2_a, rown_a = order.note(*self.rest(words_a, 1, 3, self.blocks[2:]))
        order.noted = ()
        far_b = order.note(self.send(self.both(across_b, r1_a), EDGES))
        got_a = order.note(self.send(r0_a + near_b, MIDDLE))
        tot_b = order.note(self.solve((0, 1, 2), [[own_b], [side_b], [mid_b, near_b]], None))
        order.noted = ()
        rs_a, rm_a = order.note(self.send(r2_a + got_a, EDGES), self.send(r1_a + far_b, MIDDLE))
        tot_b = self.last(across_b, far_b, tot_b)
        solved_b, words_b, r0_b = order.note(*self.first(tot_b, self.swap(tot_b)))
        r0_b, words_b, rown_a, rs_a, rm_a = order.step(r0_b, words_b, rown_a, rs_a, rm_a)
        sent_a = rown_a + rs_a + rm_a
        if prepare:
            near = order.note(self.send(r0_b, OUTWARD))
            passed_a = passed(sent_a)
            r1_b = order.note(*self.rest(words_b, 1, 1, self.blocks[2:]))
            r0_b, near, r1_b, passed_a, words_b = order.step(r0_b, near, r1_b, passed_a, words_b)
            far, got = order.note(self.send_first(r1_b, OUTWARD), self.send(r0_b + near, MIDDLE))
            r2_b, rown_b = order.note(*self.rest(words_b, 2, 2, ()))
            r2_b, got, r1_b, far = order.step(r2_b, got, r1_b, far)
            rs_b, rm_b = self.send_first(r2_b + got, EDGES), self.send(r1_b + far, MIDDLE)
        else:
            near = self.send_first(r0_b, OUTWARD, 64)
            passed_a = passed(sent_a)
            r1_b, = self.rest(words_b, 1, 1, self.blocks[2:])
            far = self.send_first(r1_b, OUTWARD)
            words_b, passed_a = lax.optimization_barrier((words_b, passed_a))
            r2_b, rown_b = self.rest(words_b, 2, 2, ())
            got = self.send(r0_b + near, MIDDLE)
            rm_b = self.send(r1_b + far, MIDDLE)
            rs_b = self.send(r2_b + got, EDGES)
        sent_b = rown_b + rs_b + rm_b
        return solved_a, sent_a, solved_b, sent_b, passed_a


def to_last(sent):
    half = sent.shape[0] // 2
    upper, lower = sent[:half], sent[half:]
    got_upper = hop(upper, ((0, 1), (2, 3)))
    got_lower = hop(lower, ((0, 2), (1, 3)))
    sum_upper = hop(upper + got_upper, ((1, 3),))
    sum_lower = hop(lower + got_lower, ((2, 3),))
    return jnp.concatenate([got_upper + sum_upper, got_lower + sum_lower], axis=0)


def shards_line(rhs, inv_factor, coupling, pattern):
    top = lax.axis_size("sec") - 1
    factor, panel = inv_factor[0], coupling[0]
    mask = jnp.repeat(pattern[0].astype(F32), panel.shape[1] // pattern.shape[2], axis=1)
    is_parent = lax.axis_index("sec") == top
    col = lax.axis_index("col")
    inner = (col != 0) & (col != lax.axis_size("col") - 1)
    flags = jnp.stack([~is_parent, is_parent, ~inner]).astype(jnp.int32)
    orders = jnp.asarray([a + b for a, b in zip(ARRIVE, LEAVE)], jnp.int32)
    meta = jnp.concatenate([flags, orders[col]])

    height = panel.shape[0] // len(LEAVE)
    per = height * mask.shape[0] // panel.shape[0]

    def late(meta):
        depth = rhs.shape[1]
        return lax.dynamic_slice(factor, (0, meta[ORDER + 3] * depth), (factor.shape[0], depth))

    def early(meta, mask, k):
        rows = lax.dynamic_slice(panel, (meta[SHARD + k] * height, 0), (height, panel.shape[1]))
        cover = lax.dynamic_slice(mask, (meta[SHARD + k] * per, 0), (per, panel.shape[1]))
        rows = rows.reshape(per, height // per, panel.shape[1]) * cover[:, None, :]
        return rows.reshape(height, panel.shape[1])

    kids = Line(0, tuple(range(top)), meta, inner, factor, panel, mask, (late, early))
    half = rhs.shape[2] // 2
    own = [rhs[0][:, :half], rhs[0][:, half:]]
    solved0, sent0, solved1, sent1, passed0 = kids.pair(own[0], own[1], lambda rows: rows, to_last)
    head = Line(1, (top,), kids.meta, inner, factor, panel, kids.mask, kids.blocks)
    psolved0, psent0, psolved1, psent1, _ = head.pair(
        own[0] - passed0, sent1, lambda sent: own[1] - to_last(sent), lambda sent: sent
    )
    pick = lambda p, c: jnp.where(is_parent, p, c)
    solution = jnp.concatenate([pick(psolved0, solved0), pick(psolved1, solved1)], axis=1)
    outgoing = jnp.concatenate([pick(psent0, sent0), pick(psent1, sent1)], axis=1)
    return solution[None], outgoing[None]


def shards_any(rhs, inv_factor, coupling, pattern):
    highest = lax.Precision.HIGHEST
    factor = inv_factor[0]
    coupling_local = coupling[0]
    occupancy = pattern[0].astype(jnp.float32)
    block_rows = coupling_local.shape[0] // occupancy.shape[0]
    block_cols = coupling_local.shape[1] // occupancy.shape[1]
    masked = (
        coupling_local.reshape(occupancy.shape[0], block_rows, occupancy.shape[1], block_cols)
        * occupancy[:, None, :, None]
    ).reshape(coupling_local.shape)
    parent_flag = lax.axis_index("sec") == lax.axis_size("sec") - 1

    def segment(rows):
        operand = lax.all_gather(rows, "col", axis=0, tiled=True)
        solved = lax.psum(jnp.dot(factor, operand, precision=highest, preferred_element_type=F32), "row")
        update = jnp.dot(masked, solved, precision=highest, preferred_element_type=F32)
        return solved, lax.psum_scatter(update, "col", scatter_dimension=0, tiled=True)

    solved_a, shares_a = segment(rhs[0])
    total = lax.psum(jnp.where(parent_flag, 0.0, shares_a), "sec")
    solved_b, shares_b = segment(rhs[0] - total)
    solution = jnp.where(parent_flag, solved_b, solved_a)
    outgoing = jnp.where(parent_flag, shares_b, shares_a)
    return (solution[None], outgoing[None])


def solution(mesh):
    placed = (
        P("sec", ("row", "col"), None),
        P("sec", "col", "row"),
        P("sec", "row", "col"),
        P("sec", "row", "col"),
    )
    line = mesh.shape["col"] == 4 and mesh.shape["row"] == 2 and mesh.shape["sec"] == 4
    return jax.shard_map(
        shards_line if line else shards_any,
        mesh=mesh,
        in_specs=placed,
        out_specs=(P("sec", "col", None), P("sec", ("row", "col"), None)),
        check_vma=False,
    )
```
